256 devices in a mesh: query: 2 (over y_hi), wide: 128 (over z, y_lo, x, core).
Axes of the slice: x: 4, y: 4 (y_hi: 2, y_lo: 2; y = y_hi * 2 + y_lo), z: 8, core: 2. Of those that a mesh axis runs over, the one named last changes fastest.
Arguments:
- queries: bfloat16 [8192, 256], P(('query', 'wide')), may hold values from -3 to 3
- items: bfloat16 [131072, 256], P('wide'), may hold values from -24 to 24
- positive_ids: int32 [8192], P(('query', 'wide')), may hold values from 0 to 131071
Outputs:
- query_grad: float32 [8192, 256], P(('query', 'wide'))
- query_loss: float32 [8192], P(('query', 'wide'))
- item_grad: float32 [131072, 256], P('wide')
The draws below stay inside these ranges and needn't reach their ends.
All inputs are finite; a program needn't handle non-finite values.
Results may differ from the reference program's by a relative error of at most 0.00085.
Values may be sent and summed in bfloat16 or wider, within the bound.
A program may use at most 64 MiB of HBM per device.

```python
import math
import jax
import jax.numpy as jnp
from jax import lax

E = 256
ITEMS = 131072
QUERIES = 8192


def touch_ends(values, rng, least, largest):
    longest = values.shape.index(max(values.shape))
    spots = []
    for shift in (0, 1):
        where = [jax.random.randint(jax.random.fold_in(rng, axis), (), 0, length) for axis, length in enumerate(values.shape)]
        where[longest] = (where[longest] + shift) % values.shape[longest]
        spots.append(tuple(where))
    return values.at[spots[0]].set(least).at[spots[1]].set(largest)


def steps_of(rng, dims, cuts, smallest, largest):
    loudness = 1.0
    for dim, shards_of in cuts:
        draws = jax.random.uniform(jax.random.fold_in(jax.random.fold_in(rng, 6), dim), (shards_of,), jnp.float32, smallest / len(cuts), largest / len(cuts))
        loudness = loudness * jnp.repeat(jnp.exp(draws), dims[dim] // shards_of).reshape((-1,) + (1,) * (len(dims) - 1 - dim))
    return loudness


def noise(own_key, dims, deviation, most, shards=(), kind=jnp.bfloat16):
    factor_of = steps_of(own_key, dims, shards, -0.22, 0.18) if shards else 1.0
    array = jax.random.normal(own_key, dims, jnp.float32) * deviation * factor_of
    return jnp.minimum(jnp.maximum(array, -most), most).astype(kind)


def setup_inputs(seed: int = 0) -> dict:
    splits = jax.random.split(jax.random.key(seed), 4)
    return {
        "queries": noise(splits[0], (QUERIES, E), 0.5, 3.0, ((0, 256),)),
        "items": noise(splits[1], (ITEMS, E), 4.0, 24.0, ((0, 128),)),
        "positive_ids": touch_ends(jax.random.randint(splits[2], (QUERIES,), 0, ITEMS), jax.random.fold_in(splits[2], 1), 0, ITEMS - 1).astype(jnp.int32),
    }


logit_scale = 0.0625
logit_shift = -2.0


def reference(queries, items, positive_ids):
    block = math.gcd(QUERIES, 512)
    blocks = queries.reshape(-1, block, E)
    targets = positive_ids.reshape(-1, block)
    column = jnp.arange(ITEMS, dtype=jnp.int32)

    def step(item_total, pair):
        rows, wanted = pair
        scores = jnp.dot(rows, items.T, preferred_element_type=jnp.float32) * logit_scale + logit_shift
        signs = jnp.where(column[None, :] == wanted[:, None], 1.0, -1.0).astype(jnp.float32)
        losses = jax.nn.softplus(-signs * scores)
        slopes = (-signs * jax.nn.sigmoid(-signs * scores)).astype(jnp.bfloat16)
        grads = jnp.dot(slopes, items, preferred_element_type=jnp.float32) * logit_scale
        item_total = item_total + jnp.dot(slopes.T, rows, preferred_element_type=jnp.float32) * logit_scale
        return item_total, (grads, jnp.sum(losses, axis=1) / ITEMS)

    start_total = jnp.zeros((ITEMS, E), jnp.float32)
    item_grad, outputs = lax.scan(step, start_total, (blocks, targets))
    query_grad = outputs[0].reshape(-1, E)
    query_loss = outputs[1].reshape(-1)
    return query_grad, query_loss, item_grad
```

```python
import functools

import jax
import jax.numpy as jnp
from jax import lax
from jax.experimental import pallas as pl
from jax.experimental.pallas import tpu as pltpu
from jax.sharding import PartitionSpec as P

MESH = pl.DeviceIdType.MESH
logit_scale = 0.0625
logit_shift = -2.0
log2e = 1.4426950408889634

NZ, NY, NX, NC = 8, 2, 4, 2
BLOCK = 32
ROWS = NZ * NY * BLOCK
TALL = ROWS + 8
ITEMS = 1024
E = 256
OFFSETS = (0, 0, 1, 1, 3, 3, 2, 2)
ORDER = (0, 1, 0, 1, 1, 0, 1, 0)


def pick(step, table):
    total = 0
    for k, value in enumerate(table):
        if value:
            total = total + value * jnp.where(step == k, 1, 0)
    return total


def compute_tile(q, ids, panel, first_item, grad_total):
    z = lax.dot_general(q, panel, (((1,), (1,)), ((), ())), preferred_element_type=jnp.float32)
    wanted = jnp.concatenate(
        [jnp.broadcast_to(ids[:, j : j + 1], (8, 128)) for j in range(ROWS // 8)], axis=0
    )
    place = wanted - first_item - lax.broadcasted_iota(jnp.int32, (ROWS, 128), 1)
    slopes = []
    product, relus = None, None
    for c in range(ITEMS // 128):
        scores = z[:, c * 128 : (c + 1) * 128] + logit_shift
        hit = place == c * 128
        v = jnp.where(hit, -scores, scores)
        e = jnp.exp2(jnp.abs(v) * (-log2e))
        u = 1.0 + e
        r = 1.0 / u
        g = jnp.where(v >= 0, r, e * r)
        slopes.append(jnp.where(hit, -g, g).astype(jnp.bfloat16))
        relu = jnp.maximum(v, 0.0)
        product = e if product is None else product * u + e
        relus = relu if relus is None else relus + relu
    slope = jnp.concatenate(slopes, axis=1)
    grads = jnp.dot(slope, panel, preferred_element_type=jnp.float32)
    grad_total[...] += lax.dot_general(
        q, slope, (((0,), (0,)), ((), ())), preferred_element_type=jnp.float32
    )
    whole = 1.0 + product
    losses = relus + jnp.log(whole) + (product - (whole - 1.0)) / whole
    return grads, losses


def kernel(
    q_ref, ids_ref, items_ref, qgrad_ref, loss_ref, igrad_ref,
    qbuf, idz, idy, idm, tiles, sib_recv, x_recv, z_send, z_recv, z_sum, y_send, y_recv,
    ig_total, ig_send, ig_recv,
    gz_s, gz_r, iz_s, iz_r, gy_s, gy_r, iy_s, iy_r, gx_s, gx_r, ix_s, ix_r, gc_s, gc_r, ic_s, ic_r,
    tc_s, tc_r, tx_s, tx_r, tz_s, tz_r, ty_s, ty_r, ig_s, ig_r,
):
    hi = lax.axis_index("query")
    w = lax.axis_index("wide")
    core, x, lo, z = w % 2, (w // 2) % 4, (w // 8) % 2, w // 16

    def at(dz=0, dy=0, dx=0, dc=0, dh=0):
        zz, yy, xx, cc, hh = (z + dz) % NZ, (lo + dy) % NY, (x + dx) % NX, (core + dc) % NC, (hi + dh) % 2
        return (hh, ((zz * NY + yy) * NX + xx) * NC + cc)

    def copy(src, dst, send, recv, to):
        return pltpu.make_async_remote_copy(
            src_ref=src, dst_ref=dst, send_sem=send, recv_sem=recv, device_id=to, device_id_type=MESH
        )

    mine = pl.ds(pl.multiple_of(lo * (NZ * BLOCK) + z * BLOCK, BLOCK), BLOCK)
    qbuf[x, core, mine] = (q_ref[...].astype(jnp.float32) * logit_scale).astype(jnp.bfloat16)
    lane = lax.broadcasted_iota(jnp.int32, (8, 128), 1)
    sub = lax.broadcasted_iota(jnp.int32, (8, 128), 0)
    padded = jnp.concatenate([ids_ref[...], jnp.zeros((1, 96), jnp.int32)], axis=1)
    wide_ids = jnp.broadcast_to(padded, (8, 128))
    own_ids = jnp.zeros((8, 128), jnp.int32)
    for k in range(4):
        part = jnp.sum(jnp.where(lane == sub + k * 8, wide_ids, 0), axis=1, keepdims=True)
        own_ids = jnp.where(lane % 4 == k, jnp.broadcast_to(part, (8, 128)), own_ids)
    idz[z] = own_ids

    barrier = pltpu.get_barrier_semaphore()
    peers = [at(dz=k) for k in range(1, NZ)] + [at(dx=k) for k in range(1, NX)]
    peers += [at(dy=1), at(dc=1), at(dh=1)]
    for peer in peers:
        pl.semaphore_signal(barrier, inc=1, device_id=peer, device_id_type=MESH)
    pl.semaphore_wait(barrier, len(peers))

    def gz(k):
        return copy(qbuf.at[x, core, mine], qbuf.at[x, core, mine], gz_s.at[k], gz_r.at[k], at(dz=k))

    def iz(k):
        return copy(idz.at[z], idz.at[z], iz_s.at[k], iz_r.at[k], at(dz=k))

    for k in (4, 3, 5, 2, 6, 1, 7):
        iz(k).start()
        gz(k).start()
    ig_total[...] = jnp.zeros_like(ig_total)
    for k in range(1, NZ):
        iz(k).wait_recv()
    half_ids = jnp.zeros((8, 128), jnp.int32)
    for k in range(NZ):
        half_ids = jnp.where(lane // 4 == lo * NZ + k, idz[k], half_ids)
    idy[0] = half_ids
    iy = copy(idy.at[0], idy.at[1], iy_s, iy_r, at(dy=1))
    iy.start()
    for k in range(1, NZ):
        gz(k).wait_recv()

    half = pl.ds(pl.multiple_of(lo * (NZ * BLOCK), NZ * BLOCK), NZ * BLOCK)
    gy = copy(qbuf.at[x, core, half], qbuf.at[x, core, half], gy_s, gy_r, at(dy=1))
    gy.start()
    iy.wait_recv()
    idm[x, core] = half_ids + idy[1]

    def gx(k):
        return copy(qbuf.at[x, core], qbuf.at[x, core], gx_s.at[k], gx_r.at[k], at(dx=k))

    def ix(k):
        return copy(idm.at[x, core], idm.at[x, core], ix_s.at[k], ix_r.at[k], at(dx=k))

    def gc(k):
        xx = (x + NX - k) % NX
        return copy(qbuf.at[xx, core], qbuf.at[xx, core], gc_s.at[k], gc_r.at[k], at(dc=1))

    def ic(k):
        xx = (x + NX - k) % NX
        return copy(idm.at[xx, core], idm.at[xx, core], ic_s.at[k], ic_r.at[k], at(dc=1))

    for k in (1, 3, 2):
        ix(k).start()
    ic(0).start()
    gy.wait_recv()
    for k in (1, 3):
        gx(k).start()
    gc(0).start()

    def arrived(k):
        ix(k).wait_recv()
        gx(k).wait_recv()
        ic(k).start()
        gc(k).start()

    def from_sib(k):
        ic(k).wait_recv()
        gc(k).wait_recv()

    def tc(d):
        return copy(tiles.at[NX + d], sib_recv.at[d], tc_s.at[d], tc_r.at[d], at(dc=1))

    def tx(d):
        return copy(tiles.at[d], x_recv.at[d - 1], tx_s.at[d - 1], tx_r.at[d - 1], at(dx=d))

    def joined(d):
        tc(d).wait_recv()
        tiles[d] = tiles[d] + sib_recv[d]
        tx(d).start()

    def step(k, _):
        @pl.when(k == 1)
        def _():
            gx(2).start()
            from_sib(0)

        @pl.when(k == 2)
        def _():
            arrived(3)

        @pl.when(k == 3)
        def _():
            arrived(1)
            from_sib(3)

        @pl.when(k == 4)
        def _():
            from_sib(1)

        @pl.when(k == 5)
        def _():
            arrived(2)
            joined(1)

        @pl.when(k == 6)
        def _():
            from_sib(2)
            joined(3)

        off = pick(k, OFFSETS)
        other = pick(k, ORDER)
        xx, cc = (x + off) % NX, (core + other) % NC
        grads, losses = compute_tile(
            qbuf[xx, cc], idm[xx, cc], items_ref[...], (w * ITEMS), ig_total
        )
        slot = other * NX + off
        tiles[slot, 0:ROWS] = grads
        sums = [
            jnp.sum(losses[b * 128 : (b + 1) * 128].T, axis=0, keepdims=True) for b in range(ROWS // 128)
        ]
        block = jnp.concatenate(sums + [jnp.zeros((8 - len(sums), 128), jnp.float32)], axis=0)
        tiles[slot, ROWS:TALL] = jnp.concatenate([block, jnp.zeros((8, 128), jnp.float32)], axis=1)

        @pl.when(other == 1)
        def _():
            tc(off).start()

        return 0

    lax.fori_loop(0, len(ORDER), step, 0)

    joined(2)

    def ig(k):
        part = pl.ds(k * 256, 256)
        return copy(ig_send.at[part], ig_recv.at[part], ig_s.at[k], ig_r.at[k], at(dh=1))

    for k in range(ITEMS // 256):
        ig_send[k * 256 : (k + 1) * 256] = ig_total[:, k * 256 : (k + 1) * 256].T
        ig(k).start()

    tc(0).wait_recv()
    for d in range(1, NX):
        tx(d).wait_recv()

    def column_sum(rows):
        total = tiles[0, rows] + sib_recv[0, rows]
        for d in range(NX - 1):
            total = total + x_recv[d, rows]
        return total

    loss_block = column_sum(pl.ds(ROWS, 8))

    def fill(k, _):
        for yy in range(NY):
            rows = pl.ds(pl.multiple_of(yy * (NZ * BLOCK) + k * BLOCK, BLOCK), BLOCK)
            z_send[k, yy * BLOCK : (yy + 1) * BLOCK] = column_sum(rows)
        z_send[k, NY * BLOCK :] = loss_block
        return 0

    def tz(k):
        return copy(z_send.at[(z + k) % NZ], z_recv.at[k - 1], tz_s.at[k - 1], tz_r.at[k - 1], at(dz=k))

    lax.fori_loop(0, NZ, fill, 0)
    for k in (4, 3, 5, 2, 6, 1, 7):
        tz(k).start()
    for k in range(1, NZ):
        tz(k).wait_recv()
    total = z_send[z]
    for k in range(NZ - 1):
        total = total + z_recv[k]
    z_sum[...] = total
    other_rows = pl.ds(pl.multiple_of((1 - lo) * BLOCK, BLOCK), BLOCK)
    own_rows = pl.ds(pl.multiple_of(lo * BLOCK, BLOCK), BLOCK)
    y_send[0:BLOCK] = z_sum[other_rows]
    y_send[BLOCK:] = z_sum[NY * BLOCK :]
    ty = copy(y_send, y_recv, ty_s, ty_r, at(dy=1))
    ty.start()
    ty.wait_recv()
    qgrad_ref[...] = (z_sum[own_rows] + y_recv[0:BLOCK]) * logit_scale
    y_recv[BLOCK:] = z_sum[NY * BLOCK :] + y_recv[BLOCK:]
    line = jnp.where(sub == lo * 2 + z // 4, y_recv[BLOCK:, 0:128], 0.0)
    line = jnp.broadcast_to(jnp.sum(line, axis=0, keepdims=True), (8, 128))
    line = pltpu.roll(line, (128 - (z % 4) * BLOCK) % 128, 1)
    loss_ref[...] = line[0:1, 0:BLOCK] * (1.0 / (ITEMS * NZ * NY * NX * NC))

    for k in range(ITEMS // 256):
        part = slice(k * 256, (k + 1) * 256)
        ig(k).wait_recv()
        igrad_ref[part] = ig_send[part] + ig_recv[part]

    for k in range(1, NZ):
        iz(k).wait_send()
        gz(k).wait_send()
        tz(k).wait_send()
    iy.wait_send()
    gy.wait_send()
    ty.wait_send()
    for k in range(1, NX):
        ix(k).wait_send()
        gx(k).wait_send()
        tx(k).wait_send()
    for k in range(NX):
        ic(k).wait_send()
        gc(k).wait_send()
        tc(k).wait_send()
        ig(k).wait_send()


def body(queries, items, positive_ids):
    dma = pltpu.SemaphoreType.DMA
    vmem = pl.BlockSpec(memory_space=pltpu.VMEM)
    f32, bf16, i32 = jnp.float32, jnp.bfloat16, jnp.int32
    qgrad, loss, igrad = pl.pallas_call(
        kernel,
        out_shape=(
            jax.ShapeDtypeStruct((BLOCK, E), f32),
            jax.ShapeDtypeStruct((1, BLOCK), f32),
            jax.ShapeDtypeStruct((ITEMS, E), f32),
        ),
        in_specs=[vmem] * 3,
        out_specs=[vmem] * 3,
        scratch_shapes=[
            pltpu.VMEM((NX, NC, ROWS, E), bf16),
            pltpu.VMEM((NZ, 8, 128), i32),
            pltpu.VMEM((2, 8, 128), i32),
            pltpu.VMEM((NX, NC, 8, 128), i32),
            pltpu.VMEM((2 * NX, TALL, E), f32),
            pltpu.VMEM((NX, TALL, E), f32),
            pltpu.VMEM((NX - 1, TALL, E), f32),
            pltpu.VMEM((NZ, NY * BLOCK + 8, E), f32),
            pltpu.VMEM((NZ - 1, NY * BLOCK + 8, E), f32),
            pltpu.VMEM((NY * BLOCK + 8, E), f32),
            pltpu.VMEM((BLOCK + 8, E), f32),
            pltpu.VMEM((BLOCK + 8, E), f32),
            pltpu.VMEM((E, ITEMS), f32),
            pltpu.VMEM((ITEMS, E), f32),
            pltpu.VMEM((ITEMS, E), f32),
            dma((NZ,)), dma((NZ,)), dma((NZ,)), dma((NZ,)),
            dma, dma, dma, dma,
            dma((NX,)), dma((NX,)), dma((NX,)), dma((NX,)),
            dma((NX,)), dma((NX,)), dma((NX,)), dma((NX,)),
            dma((NX,)), dma((NX,)),
            dma((NX - 1,)), dma((NX - 1,)),
            dma((NZ - 1,)), dma((NZ - 1,)),
            dma, dma,
            dma((ITEMS // 256,)), dma((ITEMS // 256,)),
        ],
        compiler_params=pltpu.CompilerParams(
            collective_id=0, has_side_effects=True, vmem_limit_bytes=60 * 2**20
        ),
        cost_estimate=pl.CostEstimate(
            flops=6 * NX * NC * ROWS * ITEMS * E, bytes_accessed=4 * 2**20, transcendentals=2 * NX * NC * ROWS * ITEMS
        ),
    )(queries, positive_ids.reshape(1, BLOCK), items)
    return qgrad, loss.reshape(BLOCK), igrad


def solution(mesh):
    return jax.shard_map(
        body,
        mesh=mesh,
        in_specs=(P(("query", "wide"), None), P("wide", None), P(("query", "wide"))),
        out_specs=(P(("query", "wide"), None), P(("query", "wide")), P("wide", None)),
        check_vma=False,
    )
```

```python
import jax
import jax.numpy as jnp
from jax import lax
from jax.experimental import pallas as pl
from jax.experimental.pallas import tpu as pltpu
from jax.sharding import PartitionSpec as P

MESH = pl.DeviceIdType.MESH
logit_scale = 0.0625
logit_shift = -2.0
log2e = 1.4426950408889634

NZ, NY, NX, NC = 8, 2, 4, 2
BLOCK = 32
COL = NZ * BLOCK
QCOL = COL + 16
TCOL = COL + 8
ZROWS = BLOCK + 8
ITEMS = 1024
E = 256
OFFSETS = (0, 1, 3, 2, 1, 3, 2, 0)


def pick(step, table):
    total = 0
    for k, value in enumerate(table):
        if value:
            total = total + value * jnp.where(step == k, 1, 0)
    return total


def compute_tile(q, ids, panel, first_item, grad_total):
    rows = NC * COL
    z = lax.dot_general(q, panel, (((1,), (1,)), ((), ())), preferred_element_type=jnp.float32)
    wanted = jnp.concatenate(
        [jnp.broadcast_to(ids[:, j : j + 1], (8, 128)) for j in range(rows // 8)], axis=0
    )
    place = wanted - first_item - lax.broadcasted_iota(jnp.int32, (rows, 128), 1)
    slopes = []
    product, relus = None, None
    for c in range(ITEMS // 128):
        scores = z[:, c * 128 : (c + 1) * 128] + logit_shift
        hit = place == c * 128
        v = jnp.where(hit, -scores, scores)
        e = jnp.exp2(jnp.abs(v) * (-log2e))
        u = 1.0 + e
        r = 1.0 / u
        g = jnp.where(v >= 0, r, e * r)
        slopes.append(jnp.where(hit, -g, g).astype(jnp.bfloat16))
        relu = jnp.maximum(v, 0.0)
        product = e if product is None else product * u + e
        relus = relu if relus is None else relus + relu
    slope = jnp.concatenate(slopes, axis=1)
    grads = jnp.dot(slope, panel, preferred_element_type=jnp.float32)
    grad_total[...] += lax.dot_general(
        slope, q, (((0,), (0,)), ((), ())), preferred_element_type=jnp.float32
    )
    whole = 1.0 + product
    losses = relus + jnp.log(whole) + (product - (whole - 1.0)) / whole
    return grads, losses


def kernel(
    q_ref, ids_ref, items_ref, qgrad_ref, loss_ref, ig_own, ig_other,
    qbuf, idz, tiles, sib_recv, x_recv, z_send, z_recv, y_send, y_recv, ig_total,
    gz_s, gz_r, iz_s, iz_r, gy_s, gy_r, gx_s, gx_r, ga_s, ga_r, gb_s, gb_r,
    tc_s, tc_r, tx_s, tx_r, tz_s, tz_r, ty_s, ty_r, ig_s, ig_r, out_s,
):
    hi = lax.axis_index("query")
    w = lax.axis_index("wide")
    core, x, lo, z = w % 2, (w // 2) % 4, (w // 8) % 2, w // 16

    def at(dz=0, dy=0, dx=0, dc=0, dh=0):
        zz, yy, xx, cc, hh = (z + dz) % NZ, (lo + dy) % NY, (x + dx) % NX, (core + dc) % NC, (hi + dh) % 2
        return (hh, ((zz * NY + yy) * NX + xx) * NC + cc)

    def copy(src, dst, send, recv, to):
        return pltpu.make_async_remote_copy(
            src_ref=src, dst_ref=dst, send_sem=send, recv_sem=recv, device_id=to, device_id_type=MESH
        )

    barrier = pltpu.get_barrier_semaphore()
    peers = [at(dz=k) for k in (4, 3, 5, 2, 6, 1, 7)] + [at(dx=k) for k in range(1, NX)]
    peers += [at(dy=1), at(dc=1), at(dh=1)]
    for peer in peers:
        pl.semaphore_signal(barrier, inc=1, device_id=peer, device_id_type=MESH)

    mine = pl.ds(pl.multiple_of(z * BLOCK, BLOCK), BLOCK)
    qbuf[x, lo, core, mine] = (q_ref[...].astype(jnp.float32) * logit_scale).astype(jnp.bfloat16)
    lane = lax.broadcasted_iota(jnp.int32, (8, 128), 1)
    sub = lax.broadcasted_iota(jnp.int32, (8, 128), 0)
    padded = jnp.concatenate([ids_ref[...], jnp.zeros((1, 96), jnp.int32)], axis=1)
    wide_ids = jnp.broadcast_to(padded, (8, 128))
    own_ids = jnp.zeros((8, 128), jnp.int32)
    for k in range(4):
        part = jnp.sum(jnp.where(lane == sub + k * 8, wide_ids, 0), axis=1, keepdims=True)
        own_ids = jnp.where(lane % 4 == k, jnp.broadcast_to(part, (8, 128)), own_ids)
    idz[z] = own_ids
    pl.semaphore_wait(barrier, len(peers))

    def gz(k):
        here = qbuf.at[x, lo, core, mine]
        return copy(here, here, gz_s.at[k], gz_r.at[k], at(dz=k))

    def iz(k):
        return copy(idz.at[z], idz.at[z], iz_s.at[k], iz_r.at[k], at(dz=k))

    for k in (4, 3, 5, 2, 6, 1, 7):
        iz(k).start()
        gz(k).start()
    ig_total[...] = jnp.zeros_like(ig_total)
    for k in range(1, NZ):
        iz(k).wait_recv()
    col_ids = jnp.zeros((8, 128), jnp.int32)
    for k in range(NZ):
        col_ids = jnp.where(lane // 4 == core * NZ + k, idz[k], col_ids)
    digits = [col_ids % 256, (col_ids // 256) % 256, col_ids // 65536, jnp.zeros_like(col_ids)]
    digits = [d.astype(jnp.float32) for d in digits]
    qbuf[x, lo, core, COL:QCOL] = jnp.concatenate(
        [jnp.concatenate(digits[:2], axis=1), jnp.concatenate(digits[2:], axis=1)], axis=0
    ).astype(jnp.bfloat16)
    for k in range(1, NZ):
        gz(k).wait_recv()

    def gx(k):
        here = qbuf.at[x, lo, core]
        return copy(here, here, gx_s.at[k], gx_r.at[k], at(dx=k))

    def ga(k):
        here = qbuf.at[(x + NX - k) % NX, lo, core]
        return copy(here, here, ga_s.at[k], ga_r.at[k], at(dc=1))

    def gy(k):
        here = qbuf.at[(x + NX - k) % NX, lo, core]
        return copy(here, here, gy_s.at[k], gy_r.at[k], at(dy=1))

    def gb(k):
        here = qbuf.at[(x + NX - k) % NX, 1 - lo, core]
        return copy(here, here, gb_s.at[k], gb_r.at[k], at(dc=1))

    gx(1).start()
    gx(3).start()
    ga(0).start()
    gy(0).start()

    def arrived(k):
        gx(k).wait_recv()
        ga(k).start()
        gy(k).start()

    def crossed(k):
        gy(k).wait_recv()
        gb(k).start()

    def tc(h, d):
        return copy(tiles.at[1, h, d], sib_recv.at[h, d], tc_s.at[h, d], tc_r.at[h, d], at(dc=1))

    def tx(h, d):
        return copy(tiles.at[0, h, d], x_recv.at[h, d - 1], tx_s.at[h, d], tx_r.at[h, d], at(dx=d))

    def joined(h, d):
        tc(h, d).wait_recv()
        tiles[0, h, d] = tiles[0, h, d] + sib_recv[h, d]
        tx(h, d).start()

    def step(k, _):
        @pl.when(k == 0)
        def _():
            ga(0).wait_recv()
            gx(2).start()

        @pl.when(k == 1)
        def _():
            arrived(3)
            arrived(1)
            ga(3).wait_recv()

        @pl.when(k == 2)
        def _():
            arrived(2)
            crossed(0)
            ga(1).wait_recv()

        @pl.when(k == 3)
        def _():
            joined(0, 1)
            crossed(3)
            ga(2).wait_recv()

        @pl.when(k == 4)
        def _():
            joined(0, 3)
            crossed(1)
            gb(3).wait_recv()

        @pl.when(k == 5)
        def _():
            joined(0, 2)
            crossed(2)
            gb(1).wait_recv()

        @pl.when(k == 6)
        def _():
            joined(1, 1)
            gb(2).wait_recv()

        @pl.when(k == 7)
        def _():
            joined(1, 3)
            gb(0).wait_recv()

        off = pick(k, OFFSETS)
        h = k // NX
        xx, yy = (x + off) % NX, (lo + h) % NY
        q = jnp.concatenate([qbuf[xx, yy, cc, 0:COL] for cc in range(NC)], axis=0)
        coded = (qbuf[xx, yy, 0, COL:QCOL] + qbuf[xx, yy, 1, COL:QCOL]).astype(jnp.float32)
        ids = coded[0:8, 0:128] + coded[0:8, 128:] * 256.0 + coded[8:, 0:128] * 65536.0
        grads, losses = compute_tile(q, ids.astype(jnp.int32), items_ref[...], w * ITEMS, ig_total)
        for cc in range(NC):
            whose = (core + cc) % NC
            tiles[whose, h, off, 0:COL] = grads[cc * COL : (cc + 1) * COL]
            sums = [
                jnp.sum(losses[cc * COL + b * 128 : cc * COL + (b + 1) * 128].T, axis=0, keepdims=True)
                for b in range(COL // 128)
            ]
            block = jnp.concatenate(sums + [jnp.zeros((8 - len(sums), 128), jnp.float32)], axis=0)
            tiles[whose, h, off, COL:TCOL] = jnp.concatenate(
                [block, jnp.zeros((8, 128), jnp.float32)], axis=1
            )
        tc(h, off).start()
        return 0

    lax.fori_loop(0, len(OFFSETS), step, 0)

    def ig(k):
        part = pl.ds(k * 256, 256)
        return copy(ig_total.at[part], ig_other.at[part], ig_s.at[k], ig_r.at[k], at(dh=1))

    for k in range(ITEMS // 256):
        ig(k).start()
    keep = pltpu.make_async_copy(ig_total, ig_own, out_s)
    keep.start()
    joined(1, 2)

    def tz(h, k):
        return copy(
            z_send.at[h, (z + k) % NZ], z_recv.at[h, k - 1], tz_s.at[h, k - 1], tz_r.at[h, k - 1], at(dz=k)
        )

    def along_x(h):
        tc(h, 0).wait_recv()
        for d in (1, 3, 2):
            tx(h, d).wait_recv()

        def column_sum(rows):
            total = tiles[0, h, 0, rows] + sib_recv[h, 0, rows]
            for d in range(NX - 1):
                total = total + x_recv[h, d, rows]
            return total

        loss_block = column_sum(slice(COL, TCOL))
        for k in range(NZ):
            z_send[h, k, 0:BLOCK] = column_sum(slice(k * BLOCK, (k + 1) * BLOCK))
            z_send[h, k, BLOCK:] = loss_block
        for k in (4, 3, 5, 2, 6, 1, 7):
            tz(h, k).start()

    def along_z(h):
        for k in range(1, NZ):
            tz(h, k).wait_recv()
        total = z_send[h, z]
        for k in range(NZ - 1):
            total = total + z_recv[h, k]
        return total

    along_x(0)
    along_x(1)
    own_part = along_z(0)
    y_send[...] = along_z(1)
    ty = copy(y_send, y_recv, ty_s, ty_r, at(dy=1))
    ty.start()
    ty.wait_recv()
    total = own_part + y_recv[...]
    qgrad_ref[...] = total[0:BLOCK] * logit_scale
    line = jnp.where(sub == z // 4, total[BLOCK:, 0:128], 0.0)
    line = jnp.broadcast_to(jnp.sum(line, axis=0, keepdims=True), (8, 128))
    line = pltpu.roll(line, (128 - (z % 4) * BLOCK) % 128, 1)
    loss_ref[...] = line[0:1, 0:BLOCK] * (1.0 / (ITEMS * NZ * NY * NX * NC))

    keep.wait()
    for k in range(ITEMS // 256):
        ig(k).wait_recv()

    for k in range(1, NZ):
        iz(k).wait_send()
        gz(k).wait_send()
        for h in range(NY):
            tz(h, k).wait_send()
    ty.wait_send()
    for k in range(NX):
        if k:
            gx(k).wait_send()
        ga(k).wait_send()
        gy(k).wait_send()
        gb(k).wait_send()
        for h in range(NY):
            tc(h, k).wait_send()
            if k:
                tx(h, k).wait_send()
        ig(k).wait_send()


def finish(qgrad_in, loss_in, own, other, qgrad, loss, igrad):
    igrad[...] = own[...] + other[...]

    @pl.when(pl.program_id(0) == 0)
    def _():
        qgrad[...] = qgrad_in[...]
        loss[...] = loss_in[...]


def body(queries, items, positive_ids):
    dma = pltpu.SemaphoreType.DMA
    vmem = pl.BlockSpec(memory_space=pltpu.VMEM)
    anywhere = pl.BlockSpec(memory_space=pl.ANY)
    f32, bf16, i32 = jnp.float32, jnp.bfloat16, jnp.int32
    small = (jax.ShapeDtypeStruct((BLOCK, E), f32), jax.ShapeDtypeStruct((1, BLOCK), f32))
    large = jax.ShapeDtypeStruct((ITEMS, E), f32)
    qgrad, loss, own, other = pl.pallas_call(
        kernel,
        out_shape=small + (large, large),
        in_specs=[vmem] * 3,
        out_specs=[vmem] * 2 + [anywhere] * 2,
        scratch_shapes=[
            pltpu.VMEM((NX, NY, NC, QCOL, E), bf16),
            pltpu.VMEM((NZ, 8, 128), i32),
            pltpu.VMEM((NC, NY, NX, TCOL, E), f32),
            pltpu.VMEM((NY, NX, TCOL, E), f32),
            pltpu.VMEM((NY, NX - 1, TCOL, E), f32),
            pltpu.VMEM((NY, NZ, ZROWS, E), f32),
            pltpu.VMEM((NY, NZ - 1, ZROWS, E), f32),
            pltpu.VMEM((ZROWS, E), f32),
            pltpu.VMEM((ZROWS, E), f32),
            pltpu.VMEM((ITEMS, E), f32),
            dma((NZ,)), dma((NZ,)), dma((NZ,)), dma((NZ,)),
            dma((NX,)), dma((NX,)), dma((NX,)), dma((NX,)),
            dma((NX,)), dma((NX,)), dma((NX,)), dma((NX,)),
            dma((NY, NX)), dma((NY, NX)), dma((NY, NX)), dma((NY, NX)),
            dma((NY, NZ - 1)), dma((NY, NZ - 1)),
            dma, dma,
            dma((ITEMS // 256,)), dma((ITEMS // 256,)),
            dma,
        ],
        compiler_params=pltpu.CompilerParams(
            collective_id=0, has_side_effects=True, vmem_limit_bytes=56 * 2**20
        ),
    )(queries, positive_ids.reshape(1, BLOCK), items)
    parts = 4
    slab = pl.BlockSpec((ITEMS // parts, E), lambda i: (i, 0))
    whole = [pl.BlockSpec(s.shape, lambda i: (0, 0)) for s in small]
    qgrad, loss, igrad = pl.pallas_call(
        finish,
        grid=(parts,),
        out_shape=small + (large,),
        in_specs=whole + [slab, slab],
        out_specs=whole + [slab],
    )(qgrad, loss, own, other)
    return qgrad, loss.reshape(BLOCK), igrad


def solution(mesh):
    return jax.shard_map(
        body,
        mesh=mesh,
        in_specs=(P(("query", "wide"), None), P("wide", None), P(("query", "wide"))),
        out_specs=(P(("query", "wide"), None), P(("query", "wide")), P("wide", None)),
        check_vma=False,
    )
```

```python
import jax
import jax.numpy as jnp
from jax import lax
from jax.experimental import pallas as pl
from jax.experimental.pallas import tpu as pltpu
from jax.sharding import PartitionSpec as P

MESH = pl.DeviceIdType.MESH
logit_scale = 0.0625
logit_shift = -2.0
log2e = 1.4426950408889634

NZ, NY, NX, NC = 8, 2, 4, 2
BLOCK = 32
COL = NZ * BLOCK
QCOL = COL + 16
TCOL = COL + 8
ZROWS = BLOCK + 8
ITEMS = 1024
E = 256
OFFSETS = (0, 1, 3, 2, 1, 3)
LAST = (2, 0)
HALF = ITEMS // 2


def pick(step, table):
    total = 0
    for k, value in enumerate(table):
        if value:
            total = total + value * jnp.where(step == k, 1, 0)
    return total


def compute_tile(q, ids, panel, first_item, grad_total):
    rows = NC * COL
    z = lax.dot_general(q, panel, (((1,), (1,)), ((), ())), preferred_element_type=jnp.float32)
    wanted = jnp.concatenate(
        [jnp.broadcast_to(ids[:, j : j + 1], (8, 128)) for j in range(rows // 8)], axis=0
    )
    place = wanted - first_item - lax.broadcasted_iota(jnp.int32, (rows, 128), 1)
    slopes = []
    product, relus = None, None
    for c in range(panel.shape[0] // 128):
        scores = z[:, c * 128 : (c + 1) * 128] + logit_shift
        hit = place == c * 128
        v = jnp.where(hit, -scores, scores)
        e = jnp.exp2(jnp.abs(v) * (-log2e))
        u = 1.0 + e
        r = 1.0 / u
        g = jnp.where(v >= 0, r, e * r)
        slopes.append(jnp.where(hit, -g, g).astype(jnp.bfloat16))
        relu = jnp.maximum(v, 0.0)
        product = e if product is None else product * u + e
        relus = relu if relus is None else relus + relu
    slope = jnp.concatenate(slopes, axis=1)
    grads = jnp.dot(slope, panel, preferred_element_type=jnp.float32)
    grad_total[...] += lax.dot_general(
        slope, q, (((0,), (0,)), ((), ())), preferred_element_type=jnp.float32
    )
    whole = 1.0 + product
    losses = relus + jnp.log(whole) + (product - (whole - 1.0)) / whole
    return grads, losses


def kernel(
    q_ref, ids_ref, items_ref, qgrad_ref, loss_ref, ig_own, ig_other,
    qbuf, idz, tiles, sib_recv, x_recv, z_send, z_recv, y_send, y_recv, ig_total,
    gz_s, gz_r, iz_s, iz_r, gy_s, gy_r, gx_s, gx_r, ga_s, ga_r, gb_s, gb_r,
    tc_s, tc_r, tx_s, tx_r, tz_s, tz_r, ty_s, ty_r, ig_s, ig_r, out_s,
):
    hi = lax.axis_index("query")
    w = lax.axis_index("wide")
    core, x, lo, z = lax.rem(w, 2), lax.rem(w // 2, 4), lax.rem(w // 8, 2), w // 16

    def at(dz=0, dy=0, dx=0, dc=0, dh=0):
        to = w
        if dz:
            to = to + (lax.rem(z + dz, NZ) - z) * (NY * NX * NC)
        if dy:
            to = to + (1 - 2 * lo) * (NX * NC)
        if dx:
            to = to + (lax.rem(x + dx, NX) - x) * NC
        if dc:
            to = to + (1 - 2 * core)
        return (1 - hi if dh else hi, to)

    def copy(src, dst, send, recv, to):
        return pltpu.make_async_remote_copy(
            src_ref=src, dst_ref=dst, send_sem=send, recv_sem=recv, device_id=to, device_id_type=MESH
        )

    barrier = pltpu.get_barrier_semaphore()
    peers = [at(dz=k) for k in (4, 3, 5, 2, 6, 1, 7)] + [at(dx=k) for k in range(1, NX)]
    peers += [at(dy=1), at(dc=1), at(dh=1)]
    for peer in peers:
        pl.semaphore_signal(barrier, inc=1, device_id=peer, device_id_type=MESH)

    mine = pl.ds(pl.multiple_of(z * BLOCK, BLOCK), BLOCK)
    qbuf[x, lo, core, mine] = (q_ref[...].astype(jnp.float32) * logit_scale).astype(jnp.bfloat16)
    lane = lax.broadcasted_iota(jnp.int32, (8, 128), 1)
    sub = lax.broadcasted_iota(jnp.int32, (8, 128), 0)
    padded = jnp.concatenate([ids_ref[...], jnp.zeros((1, 96), jnp.int32)], axis=1)
    wide_ids = jnp.broadcast_to(padded, (8, 128))
    own_ids = jnp.zeros((8, 128), jnp.int32)
    for k in range(4):
        part = jnp.sum(jnp.where(lane == sub + k * 8, wide_ids, 0), axis=1, keepdims=True)
        own_ids = jnp.where(lane % 4 == k, jnp.broadcast_to(part, (8, 128)), own_ids)
    idz[z] = own_ids
    pl.semaphore_wait(barrier, len(peers))

    def gz(k):
        here = qbuf.at[x, lo, core, mine]
        return copy(here, here, gz_s.at[k], gz_r.at[k], at(dz=k))

    def iz(k):
        return copy(idz.at[z], idz.at[z], iz_s.at[k], iz_r.at[k], at(dz=k))

    for k in (4, 3, 5, 2, 6, 1, 7):
        iz(k).start()
        gz(k).start()
    ig_total[...] = jnp.zeros_like(ig_total)
    for k in range(1, NZ):
        iz(k).wait_recv()
    col_ids = jnp.zeros((8, 128), jnp.int32)
    for k in range(NZ):
        col_ids = jnp.where(lane // 4 == core * NZ + k, idz[k], col_ids)
    digits = [col_ids % 256, (col_ids // 256) % 256, col_ids // 65536, jnp.zeros_like(col_ids)]
    digits = [d.astype(jnp.float32) for d in digits]
    qbuf[x, lo, core, COL:QCOL] = jnp.concatenate(
        [jnp.concatenate(digits[:2], axis=1), jnp.concatenate(digits[2:], axis=1)], axis=0
    ).astype(jnp.bfloat16)
    for k in range(1, NZ):
        gz(k).wait_recv()

    def gx(k):
        here = qbuf.at[x, lo, core]
        return copy(here, here, gx_s.at[k], gx_r.at[k], at(dx=k))

    def ga(k):
        here = qbuf.at[lax.rem(x + NX - k, NX), lo, core]
        return copy(here, here, ga_s.at[k], ga_r.at[k], at(dc=1))

    def gy(k):
        here = qbuf.at[lax.rem(x + NX - k, NX), lo, core]
        return copy(here, here, gy_s.at[k], gy_r.at[k], at(dy=1))

    def gb(k):
        here = qbuf.at[lax.rem(x + NX - k, NX), 1 - lo, core]
        return copy(here, here, gb_s.at[k], gb_r.at[k], at(dc=1))

    gx(1).start()
    gx(3).start()
    ga(0).start()
    gy(0).start()

    def arrived(k):
        gx(k).wait_recv()
        ga(k).start()
        gy(k).start()

    def crossed(k):
        gy(k).wait_recv()
        gb(k).start()

    def tc(h, d):
        return copy(tiles.at[1, h, d], sib_recv.at[h, d], tc_s.at[h, d], tc_r.at[h, d], at(dc=1))

    def tx(h, d, s):
        rows = slice(0, TCOL if s == 0 else COL)
        return copy(
            tiles.at[0, h, d, s, rows], x_recv.at[h, d - 1, s, rows],
            tx_s.at[h, d, s], tx_r.at[h, d, s], at(dx=d),
        )

    def joined(h, d):
        tc(h, d).wait_recv()
        tiles[0, h, d] = tiles[0, h, d] + sib_recv[h, d]
        for s in range(2):
            tx(h, d, s).start()

    def tz(h, k, s):
        rows = slice(0, ZROWS if s == 0 else BLOCK)
        return copy(
            z_send.at[h, s, lax.rem(z + k, NZ), rows], z_recv.at[h, s, k - 1, rows],
            tz_s.at[h, s, k - 1], tz_r.at[h, s, k - 1], at(dz=k),
        )

    def along_x(h):
        tc(h, 0).wait_recv()
        for s in range(2):
            for d in (1, 3, 2):
                tx(h, d, s).wait_recv()

            def column_sum(rows):
                total = tiles[0, h, 0, s, rows] + sib_recv[h, 0, s, rows]
                for d in range(NX - 1):
                    total = total + x_recv[h, d, s, rows]
                return total

            for k in range(NZ):
                z_send[h, s, k, 0:BLOCK] = column_sum(slice(k * BLOCK, (k + 1) * BLOCK))
            if s == 0:
                loss_block = column_sum(slice(COL, TCOL))
                for k in range(NZ):
                    z_send[h, s, k, BLOCK:] = loss_block
            for k in (4, 3, 5, 2, 6, 1, 7):
                tz(h, k, s).start()

    def column(h, off):
        xx, yy = lax.rem(x + off, NX), lax.rem(lo + h, NY)
        q = jnp.concatenate([qbuf[xx, yy, cc, 0:COL] for cc in range(NC)], axis=0)
        coded = (qbuf[xx, yy, 0, COL:QCOL] + qbuf[xx, yy, 1, COL:QCOL]).astype(jnp.float32)
        ids = coded[0:8, 0:128] + coded[0:8, 128:] * 256.0 + coded[8:, 0:128] * 65536.0
        return q, ids.astype(jnp.int32)

    def loss_rows(losses, cc):
        sums = [
            jnp.sum(losses[cc * COL + b * 128 : cc * COL + (b + 1) * 128].T, axis=0, keepdims=True)
            for b in range(COL // 128)
        ]
        return jnp.concatenate(sums + [jnp.zeros((8 - len(sums), 128), jnp.float32)], axis=0)

    def step(k, _):
        @pl.when(k == 0)
        def _():
            ga(0).wait_recv()
            gx(2).start()

        @pl.when(k == 1)
        def _():
            arrived(3)
            arrived(1)
            ga(3).wait_recv()

        @pl.when(k == 2)
        def _():
            arrived(2)
            crossed(0)
            ga(1).wait_recv()

        @pl.when(k == 3)
        def _():
            joined(0, 1)
            crossed(3)
            ga(2).wait_recv()

        @pl.when(k == 4)
        def _():
            joined(0, 3)
            crossed(1)
            gb(3).wait_recv()

        @pl.when(k == 5)
        def _():
            joined(0, 2)
            crossed(2)
            gb(1).wait_recv()

        off = pick(k, OFFSETS)
        h = k // NX
        q, ids = column(h, off)
        grads, losses = compute_tile(q, ids, items_ref[...], w * ITEMS, ig_total)
        for cc in range(NC):
            whose = lax.rem(core + cc, NC)
            for s in range(2):
                tiles[whose, h, off, s, 0:COL] = grads[cc * COL : (cc + 1) * COL, s * 128 : (s + 1) * 128]
            tiles[whose, h, off, 0, COL:TCOL] = loss_rows(losses, cc)
            tiles[whose, h, off, 1, COL:TCOL] = jnp.zeros((8, 128), jnp.float32)
        tc(h, off).start()
        return 0

    lax.fori_loop(0, len(OFFSETS), step, 0)

    def ig(k):
        part = pl.ds(k * 256, 256)
        return copy(ig_total.at[part], ig_other.at[part], ig_s.at[k], ig_r.at[k], at(dh=1))

    def late_step(k, _):
        @pl.when(k == 0)
        def _():
            joined(1, 1)
            gb(2).wait_recv()

        @pl.when(k == 1)
        def _():
            joined(1, 3)
            gb(0).wait_recv()

        @pl.when(k == 2)
        def _():
            for part in range(HALF // 256):
                ig(part).start()

        @pl.when(k == 3)
        def _():
            along_x(0)

        off = pick(k % len(LAST), LAST)
        first = pl.multiple_of((k // len(LAST)) * HALF, HALF)
        q, ids = column(1, off)
        here = pl.ds(first, HALF)
        grads, losses = compute_tile(q, ids, items_ref[here], w * ITEMS + first, ig_total.at[here])
        for cc in range(NC):
            whose = lax.rem(core + cc, NC)
            part = grads[cc * COL : (cc + 1) * COL]
            rows = loss_rows(losses, cc)

            @pl.when(k < len(LAST))
            def _():
                for s in range(2):
                    tiles[whose, 1, off, s, 0:COL] = part[:, s * 128 : (s + 1) * 128]
                tiles[whose, 1, off, 0, COL:TCOL] = rows
                tiles[whose, 1, off, 1, COL:TCOL] = jnp.zeros((8, 128), jnp.float32)

            @pl.when(k >= len(LAST))
            def _():
                for s in range(2):
                    tiles[whose, 1, off, s, 0:COL] += part[:, s * 128 : (s + 1) * 128]
                tiles[whose, 1, off, 0, COL:TCOL] += rows

        @pl.when(k >= len(LAST))
        def _():
            tc(1, off).start()

        return 0

    lax.fori_loop(0, 2 * len(LAST), late_step, 0)

    for k in range(HALF // 256, ITEMS // 256):
        ig(k).start()
    keep = pltpu.make_async_copy(ig_total, ig_own, out_s)
    keep.start()
    joined(1, 2)

    def along_z(h, s):
        rows = slice(0, ZROWS if s == 0 else BLOCK)
        for k in range(1, NZ):
            tz(h, k, s).wait_recv()
        total = z_send[h, s, z, rows]
        for k in range(NZ - 1):
            total = total + z_recv[h, s, k, rows]
        return total

    along_x(1)
    own_part = [along_z(0, s) for s in range(2)]
    for s in range(2):
        y_send[s * ZROWS : s * ZROWS + (ZROWS if s == 0 else BLOCK)] = along_z(1, s)
    ty = copy(y_send, y_recv, ty_s, ty_r, at(dy=1))
    ty.start()
    ty.wait_recv()
    left = own_part[0] + y_recv[0:ZROWS]
    qgrad_ref[:, 0:128] = left[0:BLOCK] * logit_scale
    qgrad_ref[:, 128:] = (own_part[1] + y_recv[ZROWS:]) * logit_scale
    line = jnp.where(sub == z // 4, left[BLOCK:], 0.0)
    line = jnp.broadcast_to(jnp.sum(line, axis=0, keepdims=True), (8, 128))
    line = pltpu.roll(line, lax.rem(128 - lax.rem(z, 4) * BLOCK, 128), 1)
    loss_ref[...] = line[0:1, 0:BLOCK] * (1.0 / (ITEMS * NZ * NY * NX * NC))

    keep.wait()
    for k in range(ITEMS // 256):
        ig(k).wait_recv()

    for k in range(1, NZ):
        iz(k).wait_send()
        gz(k).wait_send()
        for h in range(NY):
            for s in range(2):
                tz(h, k, s).wait_send()
    ty.wait_send()
    for k in range(NX):
        if k:
            gx(k).wait_send()
        ga(k).wait_send()
        gy(k).wait_send()
        gb(k).wait_send()
        for h in range(NY):
            tc(h, k).wait_send()
            if k:
                for s in range(2):
                    tx(h, k, s).wait_send()
        ig(k).wait_send()


def finish(qgrad_in, loss_in, own, other, qgrad, loss, igrad):
    igrad[...] = own[...] + other[...]

    @pl.when(pl.program_id(0) == 0)
    def _():
        qgrad[...] = qgrad_in[...]
        loss[...] = loss_in[...]


def body(queries, items, positive_ids):
    dma = pltpu.SemaphoreType.DMA
    vmem = pl.BlockSpec(memory_space=pltpu.VMEM)
    anywhere = pl.BlockSpec(memory_space=pl.ANY)
    f32, bf16, i32 = jnp.float32, jnp.bfloat16, jnp.int32
    small = (jax.ShapeDtypeStruct((BLOCK, E), f32), jax.ShapeDtypeStruct((1, BLOCK), f32))
    large = jax.ShapeDtypeStruct((ITEMS, E), f32)
    qgrad, loss, own, other = pl.pallas_call(
        kernel,
        out_shape=small + (large, large),
        in_specs=[vmem] * 3,
        out_specs=[vmem] * 2 + [anywhere] * 2,
        scratch_shapes=[
            pltpu.VMEM((NX, NY, NC, QCOL, E), bf16),
            pltpu.VMEM((NZ, 8, 128), i32),
            pltpu.VMEM((NC, NY, NX, 2, TCOL, 128), f32),
            pltpu.VMEM((NY, NX, 2, TCOL, 128), f32),
            pltpu.VMEM((NY, NX - 1, 2, TCOL, 128), f32),
            pltpu.VMEM((NY, 2, NZ, ZROWS, 128), f32),
            pltpu.VMEM((NY, 2, NZ - 1, ZROWS, 128), f32),
            pltpu.VMEM((ZROWS + BLOCK, 128), f32),
            pltpu.VMEM((ZROWS + BLOCK, 128), f32),
            pltpu.VMEM((ITEMS, E), f32),
            dma((NZ,)), dma((NZ,)), dma((NZ,)), dma((NZ,)),
            dma((NX,)), dma((NX,)), dma((NX,)), dma((NX,)),
            dma((NX,)), dma((NX,)), dma((NX,)), dma((NX,)),
            dma((NY, NX)), dma((NY, NX)), dma((NY, NX, 2)), dma((NY, NX, 2)),
            dma((NY, 2, NZ - 1)), dma((NY, 2, NZ - 1)),
            dma, dma,
            dma((ITEMS // 256,)), dma((ITEMS // 256,)),
            dma,
        ],
        compiler_params=pltpu.CompilerParams(
            collective_id=0, has_side_effects=True, vmem_limit_bytes=56 * 2**20
        ),
    )(queries, positive_ids.reshape(1, BLOCK), items)
    parts = 2
    slab = pl.BlockSpec((ITEMS // parts, E), lambda i: (i, 0))
    whole = [pl.BlockSpec(s.shape, lambda i: (0, 0)) for s in small]
    qgrad, loss, igrad = pl.pallas_call(
        finish,
        grid=(parts,),
        out_shape=small + (large,),
        in_specs=whole + [slab, slab],
        out_specs=whole + [slab],
    )(qgrad, loss, own, other)
    return qgrad, loss.reshape(BLOCK), igrad


def solution(mesh):
    return jax.shard_map(
        body,
        mesh=mesh,
        in_specs=(P(("query", "wide"), None), P("wide", None), P(("query", "wide"))),
        out_specs=(P(("query", "wide"), None), P(("query", "wide")), P("wide", None)),
        check_vma=False,
    )
```

```python
import jax
import jax.numpy as jnp
from jax import lax
from jax.experimental import pallas as pl
from jax.experimental.pallas import tpu as pltpu
from jax.sharding import PartitionSpec as P

MESH = pl.DeviceIdType.MESH
logit_scale = 0.0625
logit_shift = -2.0
log2e = 1.4426950408889634

NZ, NY, NX, NC = 8, 2, 4, 2
BLOCK = 32
COL = NZ * BLOCK
QCOL = COL + 16
TCOL = COL + 8
ZROWS = BLOCK + 8
ITEMS = 1024
E = 256
OFFSETS = (0, 1, 3, 2, 1, 3, 2)
LAST = (0,)
PART = 256


def pick(step, table):
    total = 0
    for k, value in enumerate(table):
        if value:
            total = total + value * jnp.where(step == k, 1, 0)
    return total


def compute_tile(q, ids, panel, first_item, grad_total):
    rows = q.shape[0]
    z = lax.dot_general(q, panel, (((1,), (1,)), ((), ())), preferred_element_type=jnp.float32)
    wanted = jnp.concatenate(
        [jnp.broadcast_to(i[:, j : j + 1], (8, 128)) for i in ids for j in range(NC * COL // 8)], axis=0
    )
    place = wanted - first_item - lax.broadcasted_iota(jnp.int32, (rows, 128), 1)
    slopes = []
    product, relus = None, None
    for c in range(panel.shape[0] // 128):
        scores = z[:, c * 128 : (c + 1) * 128] + logit_shift
        hit = place == c * 128
        sign = jnp.where(hit, -1.0, 1.0)
        v = scores * sign
        e = jnp.exp2(jnp.abs(scores) * (-log2e))
        u = 1.0 + e
        r = 1.0 / u
        g = jnp.where(v >= 0, r, e * r)
        slopes.append((g * sign).astype(jnp.bfloat16))
        relu = jnp.maximum(v, 0.0)
        product = e if product is None else product * u + e
        relus = relu if relus is None else relus + relu
    slope = jnp.concatenate(slopes, axis=1)
    grads = jnp.dot(slope, panel, preferred_element_type=jnp.float32)
    grad_total[...] += lax.dot_general(
        slope, q, (((0,), (0,)), ((), ())), preferred_element_type=jnp.float32
    )
    whole = 1.0 + product
    losses = relus + jnp.log(whole) + (product - (whole - 1.0)) / whole
    return grads, losses


def kernel(
    q_ref, ids_ref, items_ref, qgrad_ref, loss_ref, ig_own, ig_other,
    qbuf, idz, tiles, sib_recv, x_recv, z_send, z_recv, y_send, y_recv, ig_total,
    gz_s, gz_r, iz_s, iz_r, gy_s, gy_r, gx_s, gx_r, ga_s, ga_r, gb_s, gb_r,
    tc_s, tc_r, tx_s, tx_r, tz_s, tz_r, ty_s, ty_r, ig_s, ig_r, out_s,
):
    hi = lax.axis_index("query")
    w = lax.axis_index("wide")
    core, x, lo, z = lax.rem(w, 2), lax.rem(w // 2, 4), lax.rem(w // 8, 2), w // 16

    def at(dz=0, dy=0, dx=0, dc=0, dh=0):
        to = w
        if dz:
            to = to + (lax.rem(z + dz, NZ) - z) * (NY * NX * NC)
        if dy:
            to = to + (1 - 2 * lo) * (NX * NC)
        if dx:
            to = to + (lax.rem(x + dx, NX) - x) * NC
        if dc:
            to = to + (1 - 2 * core)
        return (1 - hi if dh else hi, to)

    def copy(src, dst, send, recv, to):
        return pltpu.make_async_remote_copy(
            src_ref=src, dst_ref=dst, send_sem=send, recv_sem=recv, device_id=to, device_id_type=MESH
        )

    barrier = pltpu.get_barrier_semaphore()
    peers = [at(dz=k) for k in (4, 3, 5, 2, 6, 1, 7)] + [at(dx=k) for k in range(1, NX)]
    peers += [at(dy=1), at(dc=1), at(dh=1)]
    for peer in peers:
        pl.semaphore_signal(barrier, inc=1, device_id=peer, device_id_type=MESH)

    mine = pl.ds(pl.multiple_of(z * BLOCK, BLOCK), BLOCK)
    qbuf[x, lo, core, mine] = (q_ref[...].astype(jnp.float32) * logit_scale).astype(jnp.bfloat16)
    lane = lax.broadcasted_iota(jnp.int32, (8, 128), 1)
    sub = lax.broadcasted_iota(jnp.int32, (8, 128), 0)
    padded = jnp.concatenate([ids_ref[...], jnp.zeros((1, 96), jnp.int32)], axis=1)
    wide_ids = jnp.broadcast_to(padded, (8, 128))
    own_ids = jnp.zeros((8, 128), jnp.int32)
    for k in range(4):
        part = jnp.sum(jnp.where(lane == sub + k * 8, wide_ids, 0), axis=1, keepdims=True)
        own_ids = jnp.where(lane % 4 == k, jnp.broadcast_to(part, (8, 128)), own_ids)
    idz[z] = own_ids
    pl.semaphore_wait(barrier, len(peers))

    def gz(k):
        here = qbuf.at[x, lo, core, mine]
        return copy(here, here, gz_s.at[k], gz_r.at[k], at(dz=k))

    def iz(k):
        return copy(idz.at[z], idz.at[z], iz_s.at[k], iz_r.at[k], at(dz=k))

    for k in (4, 3, 5, 2, 6, 1, 7):
        iz(k).start()
        gz(k).start()
    ig_total[...] = jnp.zeros_like(ig_total)
    for k in range(1, NZ):
        iz(k).wait_recv()
    col_ids = jnp.zeros((8, 128), jnp.int32)
    for k in range(NZ):
        col_ids = jnp.where(lane // 4 == core * NZ + k, idz[k], col_ids)
    digits = [col_ids % 256, (col_ids // 256) % 256, col_ids // 65536, jnp.zeros_like(col_ids)]
    digits = [d.astype(jnp.float32) for d in digits]
    qbuf[x, lo, core, COL:QCOL] = jnp.concatenate(
        [jnp.concatenate(digits[:2], axis=1), jnp.concatenate(digits[2:], axis=1)], axis=0
    ).astype(jnp.bfloat16)
    for k in range(1, NZ):
        gz(k).wait_recv()

    def gx(k):
        here = qbuf.at[x, lo, core]
        return copy(here, here, gx_s.at[k], gx_r.at[k], at(dx=k))

    def ga(k):
        here = qbuf.at[lax.rem(x + NX - k, NX), lo, core]
        return copy(here, here, ga_s.at[k], ga_r.at[k], at(dc=1))

    def gy(k):
        here = qbuf.at[lax.rem(x + NX - k, NX), lo, core]
        return copy(here, here, gy_s.at[k], gy_r.at[k], at(dy=1))

    def gb(k):
        here = qbuf.at[lax.rem(x + NX - k, NX), 1 - lo, core]
        return copy(here, here, gb_s.at[k], gb_r.at[k], at(dc=1))

    gx(1).start()
    gx(3).start()
    ga(0).start()
    gy(0).start()

    def arrived(k):
        gx(k).wait_recv()
        ga(k).start()
        gy(k).start()

    def crossed(k):
        gy(k).wait_recv()
        gb(k).start()

    def tc(h, d):
        return copy(tiles.at[1, h, d], sib_recv.at[h, d], tc_s.at[h, d], tc_r.at[h, d], at(dc=1))

    def tx(h, d, s):
        rows = slice(0, TCOL if s == 0 else COL)
        return copy(
            tiles.at[0, h, d, s, rows], x_recv.at[h, d - 1, s, rows],
            tx_s.at[h, d, s], tx_r.at[h, d, s], at(dx=d),
        )

    def joined(h, d):
        tc(h, d).wait_recv()
        tiles[0, h, d] = tiles[0, h, d] + sib_recv[h, d]
        for s in range(2):
            tx(h, d, s).start()

    def tz(h, k, s):
        rows = slice(0, ZROWS if s == 0 else BLOCK)
        return copy(
            z_send.at[h, s, lax.rem(z + k, NZ), rows], z_recv.at[h, s, k - 1, rows],
            tz_s.at[h, s, k - 1], tz_r.at[h, s, k - 1], at(dz=k),
        )

    def along_x(h):
        tc(h, 0).wait_recv()
        for s in range(2):
            for d in (1, 3, 2):
                tx(h, d, s).wait_recv()

            def column_sum(rows):
                total = tiles[0, h, 0, s, rows] + sib_recv[h, 0, s, rows]
                for d in range(NX - 1):
                    total = total + x_recv[h, d, s, rows]
                return total

            for k in range(NZ):
                z_send[h, s, k, 0:BLOCK] = column_sum(slice(k * BLOCK, (k + 1) * BLOCK))
            if s == 0:
                loss_block = column_sum(slice(COL, TCOL))
                for k in range(NZ):
                    z_send[h, s, k, BLOCK:] = loss_block
            for k in (4, 3, 5, 2, 6, 1, 7):
                tz(h, k, s).start()

    def column(h, off):
        xx, yy = lax.rem(x + off, NX), lax.rem(lo + h, NY)
        q = jnp.concatenate([qbuf[xx, yy, cc, 0:COL] for cc in range(NC)], axis=0)
        coded = (qbuf[xx, yy, 0, COL:QCOL] + qbuf[xx, yy, 1, COL:QCOL]).astype(jnp.float32)
        ids = coded[0:8, 0:128] + coded[0:8, 128:] * 256.0 + coded[8:, 0:128] * 65536.0
        return q, ids.astype(jnp.int32)

    def loss_rows(losses, cc):
        sums = [
            jnp.sum(losses[cc * COL + b * 128 : cc * COL + (b + 1) * 128].T, axis=0, keepdims=True)
            for b in range(COL // 128)
        ]
        return jnp.concatenate(sums + [jnp.zeros((8 - len(sums), 128), jnp.float32)], axis=0)

    def step(k, _):
        @pl.when(k == 0)
        def _():
            ga(0).wait_recv()
            gx(2).start()

        @pl.when(k == 1)
        def _():
            arrived(3)
            arrived(1)
            ga(3).wait_recv()

        @pl.when(k == 2)
        def _():
            arrived(2)
            crossed(0)
            ga(1).wait_recv()

        @pl.when(k == 3)
        def _():
            joined(0, 1)
            crossed(3)
            ga(2).wait_recv()

        @pl.when(k == 4)
        def _():
            joined(0, 3)
            crossed(1)
            gb(3).wait_recv()

        @pl.when(k == 5)
        def _():
            joined(0, 2)
            crossed(2)
            gb(1).wait_recv()

        @pl.when(k == 6)
        def _():
            joined(1, 1)
            gb(2).wait_recv()

        off = pick(k, OFFSETS)
        h = k // NX
        q, ids = column(h, off)
        grads, losses = compute_tile(q, [ids], items_ref[...], w * ITEMS, ig_total)
        for cc in range(NC):
            whose = lax.rem(core + cc, NC)
            for s in range(2):
                tiles[whose, h, off, s, 0:COL] = grads[cc * COL : (cc + 1) * COL, s * 128 : (s + 1) * 128]
            tiles[whose, h, off, 0, COL:TCOL] = loss_rows(losses, cc)
            tiles[whose, h, off, 1, COL:TCOL] = jnp.zeros((8, 128), jnp.float32)
        tc(h, off).start()
        return 0

    lax.fori_loop(0, len(OFFSETS), step, 0)

    def ig(k):
        part = pl.ds(k * 256, 256)
        return copy(ig_total.at[part], ig_other.at[part], ig_s.at[k], ig_r.at[k], at(dh=1))

    joined_at = ITEMS // PART - 1

    def late_step(k, _):
        @pl.when(k == 0)
        def _():
            joined(1, 3)
            gb(0).wait_recv()

        for part in range(1, ITEMS // PART):

            @pl.when(k == part)
            def _():
                for i in range((part - 1) * PART // 256, part * PART // 256):
                    ig(i).start()

        @pl.when(k == joined_at - 1)
        def _():
            joined(1, 2)

        @pl.when(k == joined_at)
        def _():
            along_x(0)

        first = pl.multiple_of(k * PART, PART)
        here = pl.ds(first, PART)
        pairs = [column(1, off) for off in LAST]
        q = jnp.concatenate([p[0] for p in pairs], axis=0)
        grads, losses = compute_tile(
            q, [p[1] for p in pairs], items_ref[here], w * ITEMS + first, ig_total.at[here]
        )
        for n, off in enumerate(LAST):
            for cc in range(NC):
                whose = lax.rem(core + cc, NC)
                at_row = (n * NC + cc) * COL
                part = grads[at_row : at_row + COL]
                rows = loss_rows(losses, n * NC + cc)

                @pl.when(k == 0)
                def _():
                    for s in range(2):
                        tiles[whose, 1, off, s, 0:COL] = part[:, s * 128 : (s + 1) * 128]
                    tiles[whose, 1, off, 0, COL:TCOL] = rows
                    tiles[whose, 1, off, 1, COL:TCOL] = jnp.zeros((8, 128), jnp.float32)

                @pl.when(k > 0)
                def _():
                    for s in range(2):
                        tiles[whose, 1, off, s, 0:COL] += part[:, s * 128 : (s + 1) * 128]
                    tiles[whose, 1, off, 0, COL:TCOL] += rows

        return 0

    lax.fori_loop(0, ITEMS // PART, late_step, 0)

    for off in LAST:
        tc(1, off).start()
    for k in range((ITEMS - PART) // 256, ITEMS // 256):
        ig(k).start()
    keep = pltpu.make_async_copy(ig_total, ig_own, out_s)
    keep.start()

    def along_z(h, s):
        rows = slice(0, ZROWS if s == 0 else BLOCK)
        for k in range(1, NZ):
            tz(h, k, s).wait_recv()
        total = z_send[h, s, z, rows]
        for k in range(NZ - 1):
            total = total + z_recv[h, s, k, rows]
        return total

    along_x(1)
    own_part = [along_z(0, s) for s in range(2)]
    for s in range(2):
        y_send[s * ZROWS : s * ZROWS + (ZROWS if s == 0 else BLOCK)] = along_z(1, s)
    ty = copy(y_send, y_recv, ty_s, ty_r, at(dy=1))
    ty.start()
    ty.wait_recv()
    left = own_part[0] + y_recv[0:ZROWS]
    qgrad_ref[:, 0:128] = left[0:BLOCK] * logit_scale
    qgrad_ref[:, 128:] = (own_part[1] + y_recv[ZROWS:]) * logit_scale
    line = jnp.where(sub == z // 4, left[BLOCK:], 0.0)
    line = jnp.broadcast_to(jnp.sum(line, axis=0, keepdims=True), (8, 128))
    line = pltpu.roll(line, lax.rem(128 - lax.rem(z, 4) * BLOCK, 128), 1)
    loss_ref[...] = line[0:1, 0:BLOCK] * (1.0 / (ITEMS * NZ * NY * NX * NC))

    keep.wait()
    for k in range(ITEMS // 256):
        ig(k).wait_recv()

    for k in range(1, NZ):
        iz(k).wait_send()
        gz(k).wait_send()
        for h in range(NY):
            for s in range(2):
                tz(h, k, s).wait_send()
    ty.wait_send()
    for k in range(NX):
        if k:
            gx(k).wait_send()
        ga(k).wait_send()
        gy(k).wait_send()
        gb(k).wait_send()
        for h in range(NY):
            tc(h, k).wait_send()
            if k:
                for s in range(2):
                    tx(h, k, s).wait_send()
        ig(k).wait_send()


def finish(qgrad_in, loss_in, own, other, qgrad, loss, igrad):
    igrad[...] = own[...] + other[...]

    @pl.when(pl.program_id(0) == 0)
    def _():
        qgrad[...] = qgrad_in[...]
        loss[...] = loss_in[...]


def body(queries, items, positive_ids):
    dma = pltpu.SemaphoreType.DMA
    vmem = pl.BlockSpec(memory_space=pltpu.VMEM)
    anywhere = pl.BlockSpec(memory_space=pl.ANY)
    f32, bf16, i32 = jnp.float32, jnp.bfloat16, jnp.int32
    small = (jax.ShapeDtypeStruct((BLOCK, E), f32), jax.ShapeDtypeStruct((1, BLOCK), f32))
    large = jax.ShapeDtypeStruct((ITEMS, E), f32)
    qgrad, loss, own, other = pl.pallas_call(
        kernel,
        out_shape=small + (large, large),
        in_specs=[vmem] * 3,
        out_specs=[vmem] * 2 + [anywhere] * 2,
        scratch_shapes=[
            pltpu.VMEM((NX, NY, NC, QCOL, E), bf16),
            pltpu.VMEM((NZ, 8, 128), i32),
            pltpu.VMEM((NC, NY, NX, 2, TCOL, 128), f32),
            pltpu.VMEM((NY, NX, 2, TCOL, 128), f32),
            pltpu.VMEM((NY, NX - 1, 2, TCOL, 128), f32),
            pltpu.VMEM((NY, 2, NZ, ZROWS, 128), f32),
            pltpu.VMEM((NY, 2, NZ - 1, ZROWS, 128), f32),
            pltpu.VMEM((ZROWS + BLOCK, 128), f32),
            pltpu.VMEM((ZROWS + BLOCK, 128), f32),
            pltpu.VMEM((ITEMS, E), f32),
            dma((NZ,)), dma((NZ,)), dma((NZ,)), dma((NZ,)),
            dma((NX,)), dma((NX,)), dma((NX,)), dma((NX,)),
            dma((NX,)), dma((NX,)), dma((NX,)), dma((NX,)),
            dma((NY, NX)), dma((NY, NX)), dma((NY, NX, 2)), dma((NY, NX, 2)),
            dma((NY, 2, NZ - 1)), dma((NY, 2, NZ - 1)),
            dma, dma,
            dma((ITEMS // 256,)), dma((ITEMS // 256,)),
            dma,
        ],
        compiler_params=pltpu.CompilerParams(
            collective_id=0, has_side_effects=True, vmem_limit_bytes=56 * 2**20
        ),
    )(queries, positive_ids.reshape(1, BLOCK), items)
    parts = 2
    slab = pl.BlockSpec((ITEMS // parts, E), lambda i: (i, 0))
    whole = [pl.BlockSpec(s.shape, lambda i: (0, 0)) for s in small]
    qgrad, loss, igrad = pl.pallas_call(
        finish,
        grid=(parts,),
        out_shape=small + (large,),
        in_specs=whole + [slab, slab],
        out_specs=whole + [slab],
    )(qgrad, loss, own, other)
    return qgrad, loss.reshape(BLOCK), igrad


def solution(mesh):
    return jax.shard_map(
        body,
        mesh=mesh,
        in_specs=(P(("query", "wide"), None), P("wide", None), P(("query", "wide"))),
        out_specs=(P(("query", "wide"), None), P(("query", "wide")), P("wide", None)),
        check_vma=False,
    )
```

```python
import jax
import jax.numpy as jnp
from jax import lax
from jax.experimental import pallas as pl
from jax.experimental.pallas import tpu as pltpu
from jax.sharding import PartitionSpec as P

MESH = pl.DeviceIdType.MESH
logit_scale = 0.0625
logit_shift = -2.0
log2e = 1.4426950408889634

NZ, NY, NX, NC = 8, 2, 4, 2
BLOCK = 32
COL = NZ * BLOCK
QCOL = COL + 16
TCOL = COL + 8
ZROWS = BLOCK + 8
ITEMS = 1024
E = 256
OFFSETS = (0, 1, 3, 2, 1, 3)
LAST = (2, 0)
HALF = ITEMS // 2


def pick(step, table):
    total = 0
    for k, value in enumerate(table):
        if value:
            total = total + value * jnp.where(step == k, 1, 0)
    return total


def compute_tile(q, ids, panel, first_item, grad_total):
    rows = NC * COL
    z = lax.dot_general(q, panel, (((1,), (1,)), ((), ())), preferred_element_type=jnp.float32)
    wanted = jnp.concatenate(
        [jnp.broadcast_to(ids[:, j : j + 1], (8, 128)) for j in range(rows // 8)], axis=0
    )
    place = wanted - first_item - lax.broadcasted_iota(jnp.int32, (rows, 128), 1)
    slopes = []
    product, relus = None, None
    for c in range(panel.shape[0] // 128):
        scores = z[:, c * 128 : (c + 1) * 128] + logit_shift
        hit = place == c * 128
        sign = jnp.where(hit, -1.0, 1.0)
        v = scores * sign
        e = jnp.exp2(jnp.abs(scores) * (-log2e))
        u = 1.0 + e
        r = 1.0 / u
        g = jnp.where(v >= 0, r, e * r)
        slopes.append((g * sign).astype(jnp.bfloat16))
        relu = jnp.maximum(v, 0.0)
        product = e if product is None else product * u + e
        relus = relu if relus is None else relus + relu
    slope = jnp.concatenate(slopes, axis=1)
    grads = jnp.dot(slope, panel, preferred_element_type=jnp.float32)
    grad_total[...] += lax.dot_general(
        slope, q, (((0,), (0,)), ((), ())), preferred_element_type=jnp.float32
    )
    whole = 1.0 + product
    losses = relus + jnp.log(whole) + (product - (whole - 1.0)) / whole
    return grads, losses


def kernel(
    q_ref, ids_ref, items_ref, qgrad_ref, loss_ref, ig_own, ig_other,
    qbuf, idz, tiles, sib_recv, x_recv, z_send, z_recv, y_send, y_recv, ig_total,
    gz_s, gz_r, iz_s, iz_r, gy_s, gy_r, gx_s, gx_r, ga_s, ga_r, gb_s, gb_r,
    tc_s, tc_r, tx_s, tx_r, tz_s, tz_r, ty_s, ty_r, ig_s, ig_r, out_s,
):
    hi = lax.axis_index("query")
    w = lax.axis_index("wide")
    core, x, lo, z = lax.rem(w, 2), lax.rem(w // 2, 4), lax.rem(w // 8, 2), w // 16

    def at(dz=0, dy=0, dx=0, dc=0, dh=0):
        to = w
        if dz:
            to = to + (lax.rem(z + dz, NZ) - z) * (NY * NX * NC)
        if dy:
            to = to + (1 - 2 * lo) * (NX * NC)
        if dx:
            to = to + (lax.rem(x + dx, NX) - x) * NC
        if dc:
            to = to + (1 - 2 * core)
        return (1 - hi if dh else hi, to)

    def copy(src, dst, send, recv, to):
        return pltpu.make_async_remote_copy(
            src_ref=src, dst_ref=dst, send_sem=send, recv_sem=recv, device_id=to, device_id_type=MESH
        )

    barrier = pltpu.get_barrier_semaphore()
    peers = [at(dz=k) for k in (4, 3, 5, 2, 6, 1, 7)] + [at(dx=k) for k in range(1, NX)]
    peers += [at(dy=1), at(dc=1), at(dh=1)]
    for peer in peers:
        pl.semaphore_signal(barrier, inc=1, device_id=peer, device_id_type=MESH)

    mine = pl.ds(pl.multiple_of(z * BLOCK, BLOCK), BLOCK)
    qbuf[x, lo, core, mine] = (q_ref[...].astype(jnp.float32) * logit_scale).astype(jnp.bfloat16)
    lane = lax.broadcasted_iota(jnp.int32, (8, 128), 1)
    sub = lax.broadcasted_iota(jnp.int32, (8, 128), 0)
    padded = jnp.concatenate([ids_ref[...], jnp.zeros((1, 96), jnp.int32)], axis=1)
    wide_ids = jnp.broadcast_to(padded, (8, 128))
    own_ids = jnp.zeros((8, 128), jnp.int32)
    for k in range(4):
        part = jnp.sum(jnp.where(lane == sub + k * 8, wide_ids, 0), axis=1, keepdims=True)
        own_ids = jnp.where(lane % 4 == k, jnp.broadcast_to(part, (8, 128)), own_ids)
    idz[z] = own_ids
    pl.semaphore_wait(barrier, len(peers))

    def gz(k):
        here = qbuf.at[x, lo, core, mine]
        return copy(here, here, gz_s.at[k], gz_r.at[k], at(dz=k))

    def iz(k):
        return copy(idz.at[z], idz.at[z], iz_s.at[k], iz_r.at[k], at(dz=k))

    for k in (4, 3, 5, 2, 6, 1, 7):
        iz(k).start()
        gz(k).start()
    ig_total[...] = jnp.zeros_like(ig_total)
    for k in range(1, NZ):
        iz(k).wait_recv()
    col_ids = jnp.zeros((8, 128), jnp.int32)
    for k in range(NZ):
        col_ids = jnp.where(lane // 4 == core * NZ + k, idz[k], col_ids)
    digits = [col_ids % 256, (col_ids // 256) % 256, col_ids // 65536, jnp.zeros_like(col_ids)]
    digits = [d.astype(jnp.float32) for d in digits]
    qbuf[x, lo, core, COL:QCOL] = jnp.concatenate(
        [jnp.concatenate(digits[:2], axis=1), jnp.concatenate(digits[2:], axis=1)], axis=0
    ).astype(jnp.bfloat16)
    for k in range(1, NZ):
        gz(k).wait_recv()

    def gx(k):
        here = qbuf.at[x, lo, core]
        return copy(here, here, gx_s.at[k], gx_r.at[k], at(dx=k))

    def ga(k):
        here = qbuf.at[lax.rem(x + NX - k, NX), lo, core]
        return copy(here, here, ga_s.at[k], ga_r.at[k], at(dc=1))

    def gy(k):
        here = qbuf.at[lax.rem(x + NX - k, NX), lo, core]
        return copy(here, here, gy_s.at[k], gy_r.at[k], at(dy=1))

    def gb(k):
        here = qbuf.at[lax.rem(x + NX - k, NX), 1 - lo, core]
        return copy(here, here, gb_s.at[k], gb_r.at[k], at(dc=1))

    gx(1).start()
    gx(3).start()
    ga(0).start()
    gy(0).start()

    def arrived(k):
        gx(k).wait_recv()
        ga(k).start()
        gy(k).start()

    def crossed(k):
        gy(k).wait_recv()
        gb(k).start()

    def tc(h, d):
        return copy(tiles.at[1, h, d], sib_recv.at[h, d], tc_s.at[h, d], tc_r.at[h, d], at(dc=1))

    def tx(h, d, s):
        rows = slice(0, TCOL if s == 0 else COL)
        return copy(
            tiles.at[0, h, d, s, rows], x_recv.at[h, d - 1, s, rows],
            tx_s.at[h, d, s], tx_r.at[h, d, s], at(dx=d),
        )

    def joined(h, d):
        tc(h, d).wait_recv()
        tiles[0, h, d] = tiles[0, h, d] + sib_recv[h, d]
        for s in range(2):
            tx(h, d, s).start()

    def tz(h, k, s):
        rows = slice(0, ZROWS if s == 0 else BLOCK)
        return copy(
            z_send.at[h, s, lax.rem(z + k, NZ), rows], z_recv.at[h, s, k - 1, rows],
            tz_s.at[h, s, k - 1], tz_r.at[h, s, k - 1], at(dz=k),
        )

    def along_x(h):
        tc(h, 0).wait_recv()
        for s in range(2):
            for d in (1, 3, 2):
                tx(h, d, s).wait_recv()

            def column_sum(rows):
                total = tiles[0, h, 0, s, rows] + sib_recv[h, 0, s, rows]
                for d in range(NX - 1):
                    total = total + x_recv[h, d, s, rows]
                return total

            for k in range(NZ):
                z_send[h, s, k, 0:BLOCK] = column_sum(slice(k * BLOCK, (k + 1) * BLOCK))
            if s == 0:
                loss_block = column_sum(slice(COL, TCOL))
                for k in range(NZ):
                    z_send[h, s, k, BLOCK:] = loss_block
            for k in (4, 3, 5, 2, 6, 1, 7):
                tz(h, k, s).start()

    def column(h, off):
        xx, yy = lax.rem(x + off, NX), lax.rem(lo + h, NY)
        q = jnp.concatenate([qbuf[xx, yy, cc, 0:COL] for cc in range(NC)], axis=0)
        coded = (qbuf[xx, yy, 0, COL:QCOL] + qbuf[xx, yy, 1, COL:QCOL]).astype(jnp.float32)
        ids = coded[0:8, 0:128] + coded[0:8, 128:] * 256.0 + coded[8:, 0:128] * 65536.0
        return q, ids.astype(jnp.int32)

    def loss_rows(losses, cc):
        sums = [
            jnp.sum(losses[cc * COL + b * 128 : cc * COL + (b + 1) * 128].T, axis=0, keepdims=True)
            for b in range(COL // 128)
        ]
        return jnp.concatenate(sums + [jnp.zeros((8 - len(sums), 128), jnp.float32)], axis=0)

    def step(k, _):
        @pl.when(k == 0)
        def _():
            ga(0).wait_recv()
            gx(2).start()

        @pl.when(k == 1)
        def _():
            arrived(3)
            arrived(1)
            ga(3).wait_recv()

        @pl.when(k == 2)
        def _():
            arrived(2)
            crossed(0)
            ga(1).wait_recv()

        @pl.when(k == 3)
        def _():
            joined(0, 1)
            crossed(3)
            ga(2).wait_recv()

        @pl.when(k == 4)
        def _():
            joined(0, 3)
            crossed(1)
            gb(3).wait_recv()

        @pl.when(k == 5)
        def _():
            joined(0, 2)
            crossed(2)
            gb(1).wait_recv()

        off = pick(k, OFFSETS)
        h = k // NX
        q, ids = column(h, off)
        grads, losses = compute_tile(q, ids, items_ref[...], w * ITEMS, ig_total)
        for cc in range(NC):
            whose = lax.rem(core + cc, NC)
            for s in range(2):
                tiles[whose, h, off, s, 0:COL] = grads[cc * COL : (cc + 1) * COL, s * 128 : (s + 1) * 128]
            tiles[whose, h, off, 0, COL:TCOL] = loss_rows(losses, cc)
            tiles[whose, h, off, 1, COL:TCOL] = jnp.zeros((8, 128), jnp.float32)
        tc(h, off).start()
        return 0

    lax.fori_loop(0, len(OFFSETS), step, 0)

    def ig(k):
        part = pl.ds(k * 256, 256)
        return copy(ig_total.at[part], ig_other.at[part], ig_s.at[k], ig_r.at[k], at(dh=1))

    def late_step(k, _):
        @pl.when(k == 0)
        def _():
            joined(1, 1)
            gb(2).wait_recv()

        @pl.when(k == 1)
        def _():
            joined(1, 3)
            gb(0).wait_recv()

        @pl.when(k == 2)
        def _():
            for part in range(HALF // 256):
                ig(part).start()

        @pl.when(k == 3)
        def _():
            along_x(0)

        off = pick(k % len(LAST), LAST)
        first = pl.multiple_of((k // len(LAST)) * HALF, HALF)
        q, ids = column(1, off)
        here = pl.ds(first, HALF)
        grads, losses = compute_tile(q, ids, items_ref[here], w * ITEMS + first, ig_total.at[here])
        for cc in range(NC):
            whose = lax.rem(core + cc, NC)
            part = grads[cc * COL : (cc + 1) * COL]
            rows = loss_rows(losses, cc)

            @pl.when(k < len(LAST))
            def _():
                for s in range(2):
                    tiles[whose, 1, off, s, 0:COL] = part[:, s * 128 : (s + 1) * 128]
                tiles[whose, 1, off, 0, COL:TCOL] = rows
                tiles[whose, 1, off, 1, COL:TCOL] = jnp.zeros((8, 128), jnp.float32)

            @pl.when(k >= len(LAST))
            def _():
                for s in range(2):
                    tiles[whose, 1, off, s, 0:COL] += part[:, s * 128 : (s + 1) * 128]
                tiles[whose, 1, off, 0, COL:TCOL] += rows

        @pl.when(k >= len(LAST))
        def _():
            tc(1, off).start()

        return 0

    lax.fori_loop(0, 2 * len(LAST), late_step, 0)

    joined(1, 2)
    for k in range(HALF // 256, ITEMS // 256):
        ig(k).start()
    keep = pltpu.make_async_copy(ig_total, ig_own, out_s)
    keep.start()

    def along_z(h, s):
        rows = slice(0, ZROWS if s == 0 else BLOCK)
        for k in range(1, NZ):
            tz(h, k, s).wait_recv()
        total = z_send[h, s, z, rows]
        for k in range(NZ - 1):
            total = total + z_recv[h, s, k, rows]
        return total

    along_x(1)
    own_part = [along_z(0, s) for s in range(2)]
    for s in range(2):
        y_send[s * ZROWS : s * ZROWS + (ZROWS if s == 0 else BLOCK)] = along_z(1, s)
    ty = copy(y_send, y_recv, ty_s, ty_r, at(dy=1))
    ty.start()
    ty.wait_recv()
    left = own_part[0] + y_recv[0:ZROWS]
    qgrad_ref[:, 0:128] = left[0:BLOCK] * logit_scale
    qgrad_ref[:, 128:] = (own_part[1] + y_recv[ZROWS:]) * logit_scale
    line = jnp.where(sub == z // 4, left[BLOCK:], 0.0)
    line = jnp.broadcast_to(jnp.sum(line, axis=0, keepdims=True), (8, 128))
    line = pltpu.roll(line, lax.rem(128 - lax.rem(z, 4) * BLOCK, 128), 1)
    loss_ref[...] = line[0:1, 0:BLOCK] * (1.0 / (ITEMS * NZ * NY * NX * NC))

    keep.wait()
    for k in range(ITEMS // 256):
        ig(k).wait_recv()

    for k in range(1, NZ):
        iz(k).wait_send()
        gz(k).wait_send()
        for h in range(NY):
            for s in range(2):
                tz(h, k, s).wait_send()
    ty.wait_send()
    for k in range(NX):
        if k:
            gx(k).wait_send()
        ga(k).wait_send()
        gy(k).wait_send()
        gb(k).wait_send()
        for h in range(NY):
            tc(h, k).wait_send()
            if k:
                for s in range(2):
                    tx(h, k, s).wait_send()
        ig(k).wait_send()


def finish(qgrad_in, loss_in, own, other, qgrad, loss, igrad):
    igrad[...] = own[...] + other[...]

    @pl.when(pl.program_id(0) == 0)
    def _():
        qgrad[...] = qgrad_in[...]
        loss[...] = loss_in[...]


def body(queries, items, positive_ids):
    dma = pltpu.SemaphoreType.DMA
    vmem = pl.BlockSpec(memory_space=pltpu.VMEM)
    anywhere = pl.BlockSpec(memory_space=pl.ANY)
    f32, bf16, i32 = jnp.float32, jnp.bfloat16, jnp.int32
    small = (jax.ShapeDtypeStruct((BLOCK, E), f32), jax.ShapeDtypeStruct((1, BLOCK), f32))
    large = jax.ShapeDtypeStruct((ITEMS, E), f32)
    qgrad, loss, own, other = pl.pallas_call(
        kernel,
        out_shape=small + (large, large),
        in_specs=[vmem] * 3,
        out_specs=[vmem] * 2 + [anywhere] * 2,
        scratch_shapes=[
            pltpu.VMEM((NX, NY, NC, QCOL, E), bf16),
            pltpu.VMEM((NZ, 8, 128), i32),
            pltpu.VMEM((NC, NY, NX, 2, TCOL, 128), f32),
            pltpu.VMEM((NY, NX, 2, TCOL, 128), f32),
            pltpu.VMEM((NY, NX - 1, 2, TCOL, 128), f32),
            pltpu.VMEM((NY, 2, NZ, ZROWS, 128), f32),
            pltpu.VMEM((NY, 2, NZ - 1, ZROWS, 128), f32),
            pltpu.VMEM((ZROWS + BLOCK, 128), f32),
            pltpu.VMEM((ZROWS + BLOCK, 128), f32),
            pltpu.VMEM((ITEMS, E), f32),
            dma((NZ,)), dma((NZ,)), dma((NZ,)), dma((NZ,)),
            dma((NX,)), dma((NX,)), dma((NX,)), dma((NX,)),
            dma((NX,)), dma((NX,)), dma((NX,)), dma((NX,)),
            dma((NY, NX)), dma((NY, NX)), dma((NY, NX, 2)), dma((NY, NX, 2)),
            dma((NY, 2, NZ - 1)), dma((NY, 2, NZ - 1)),
            dma, dma,
            dma((ITEMS // 256,)), dma((ITEMS // 256,)),
            dma,
        ],
        compiler_params=pltpu.CompilerParams(
            collective_id=0, has_side_effects=True, vmem_limit_bytes=56 * 2**20
        ),
    )(queries, positive_ids.reshape(1, BLOCK), items)
    parts = 2
    slab = pl.BlockSpec((ITEMS // parts, E), lambda i: (i, 0))
    whole = [pl.BlockSpec(s.shape, lambda i: (0, 0)) for s in small]
    qgrad, loss, igrad = pl.pallas_call(
        finish,
        grid=(parts,),
        out_shape=small + (large,),
        in_specs=whole + [slab, slab],
        out_specs=whole + [slab],
    )(qgrad, loss, own, other)
    return qgrad, loss.reshape(BLOCK), igrad


def solution(mesh):
    return jax.shard_map(
        body,
        mesh=mesh,
        in_specs=(P(("query", "wide"), None), P("wide", None), P(("query", "wide"))),
        out_specs=(P(("query", "wide"), None), P(("query", "wide")), P("wide", None)),
        check_vma=False,
    )
```
